32 devices in a mesh: dp: 8 (over y, x, core), tensor: 4 (over z).
Axes of the slice: x: 2, y: 2, z: 4, core: 2. Of those that a mesh axis runs over, the one named last changes fastest.
Arguments:
- residual_in: bfloat16 [4096, 1024], P(('dp', 'tensor')), may hold values from -6 to 6
- norm1_gain: float32 [1024], replicated, may hold values from 0.25 to 1.75
- w_query: bfloat16 [1024, 1024], P('dp', 'tensor'), may hold values from -0.1875 to 0.1875
- key_weight: bfloat16 [1024, 512], P('dp', 'tensor'), may hold values from -0.1875 to 0.1875
- value_weight: bfloat16 [1024, 512], P('dp', 'tensor'), may hold values from -0.1875 to 0.1875
- w_out: bfloat16 [1024, 1024], P('dp', 'tensor'), may hold values from -0.5 to 0.5
- norm2_gain: float32 [1024], replicated, may hold values from 0.25 to 1.75
- w_gate: bfloat16 [16, 1024, 512], P(None, 'dp', 'tensor'), may hold values from -0.1875 to 0.1875
- w_up: bfloat16 [16, 1024, 512], P(None, 'dp', 'tensor'), may hold values from -0.1875 to 0.1875
- w_down: bfloat16 [16, 1024, 512], P(None, 'dp', 'tensor'), may hold values from -0.75 to 0.75
- expert_ids: int32 [4096, 8], P('dp'), may hold values from 0 to 15, all different within a row; in each aligned block of 512 rows (0 to 511, 512 to 1023, ...) at most 288 rows name the same one
- gate_weights: float32 [4096, 8], P('dp'), may hold values from 0.06 to 0.25
- out_grad: bfloat16 [4096, 1024], P(('dp', 'tensor')), may hold values from -6 to 6
Outputs:
- residual_out: bfloat16 [4096, 1024], P(('dp', 'tensor'))
- input_grad: float32 [4096, 1024], P(('dp', 'tensor'))
- norm1_gain_grad: float32 [1024], replicated
- w_query_grad: float32 [1024, 1024], P('dp', 'tensor')
- w_key_grad: float32 [1024, 512], P('dp', 'tensor')
- w_value_grad: float32 [1024, 512], P('dp', 'tensor')
- w_out_grad: float32 [1024, 1024], P('dp', 'tensor')
- norm2_gain_grad: float32 [1024], replicated
- w_gate_grad: float32 [16, 1024, 512], P(None, 'dp', 'tensor')
- w_up_grad: float32 [16, 1024, 512], P(None, 'dp', 'tensor')
- w_down_grad: float32 [16, 1024, 512], P(None, 'dp', 'tensor')
The draws below stay inside these ranges and needn't reach their ends.
Inputs may be any that keep to these rules, and one draw needn't show every extreme that they name: `expert_ids`: each row names 8 different experts. Among the 512 rows of one index of dp no expert is named by more than 288 rows.
All inputs are finite; a program needn't handle non-finite values.
Results may differ from the reference program's by a relative error of at most 0.013.
Values may be sent and summed in bfloat16 or wider, within the bound.
A program may use at most 192 MiB of HBM per device.

```python
import math
import jax
import jax.numpy as jnp
import numpy as np
from jax import lax

MODEL_WIDTH = 1024
QUERY_HEADS = 16
KEY_VALUE_HEADS = 8
HEAD_SIZE = 64
E = 16
FF = 512
TOP = 8
LEN = 512
SEQ_GROUP = 1
GT = 512
TOKENS = 4096
CAP = 288
N_DP = 8


def raised(values, key, source, target, blocks, factor):
    owner, partner = [(jnp.arange(values.shape[dim]) // (values.shape[dim] // blocks)).reshape([-1 if axis == dim else 1 for axis in range(values.ndim)]) for dim in (source, target)]
    chosen = jax.random.permutation(key, blocks)[partner]
    strong = (owner == chosen) | (owner == (partner + blocks // 2) % blocks)
    return jnp.where(strong, factor * values, values)


def shard_levels(own_key, dims, cuts, low, high):
    def one(axis_at, shards_of):
        steps = jax.random.uniform(jax.random.fold_in(jax.random.fold_in(own_key, 6), axis_at), (shards_of,), jnp.float32, low / len(cuts), high / len(cuts))
        return jnp.repeat(jnp.exp(steps), dims[axis_at] // shards_of).reshape((-1,) + (1,) * (len(dims) - axis_at - 1))

    gain = one(*cuts[0])
    for cut in cuts[1:]:
        gain = gain * one(*cut)
    return gain


def routed_block(key, own, number, rows, amount, top, most, lean):
    ranking = jax.random.permutation(key, amount)
    crowded, ordinary = load_shares(amount, rows * top, most, lean, True), load_shares(amount, rows * top, most, lean, False)
    places = jnp.arange(amount)

    def named(sizes, rotation):
        used = int((sizes > 0).sum())
        fixed = max(1, used // 4)
        shifted = fixed + (places - fixed + rotation * (used - fixed)) % max(1, amount - fixed)
        return jnp.zeros((amount,), jnp.int32).at[ranking[jnp.where(places < fixed, places, shifted)]].set(jnp.asarray(sizes, jnp.int32))

    sizes = jnp.where(number % 4 == 0, named(crowded, number // 4), named(ordinary, number - number // 4 - 1))
    mixed = jax.random.permutation(jax.random.fold_in(own, 3), amount)
    source_of, sink = mixed[0:amount // 2 * 2:2], mixed[1:amount // 2 * 2:2]
    margin = jnp.minimum(sizes[source_of] - 1, most - sizes[sink]) // 2
    margin = jnp.where((source_of == ranking[0]) | (sink == ranking[0]) | (sizes[sink] == 0), 0, jnp.maximum(margin, 0))
    shifted = jax.random.randint(jax.random.fold_in(own, 4), (amount // 2,), 0, 1 << 20) % (margin + 1)
    sizes = sizes.at[source_of].add(-shifted).at[sink].add(shifted)
    labels = jnp.searchsorted(jnp.cumsum(sizes), jnp.arange(rows * top), side="right").astype(jnp.int32)
    listing = labels.reshape(top, rows).T
    listing = listing[jax.random.permutation(jax.random.fold_in(own, 1), rows)]
    rotation = jax.random.randint(jax.random.fold_in(own, 2), (rows, 1), 0, top)
    return jnp.take_along_axis(listing, (jnp.arange(top)[None, :] + rotation) % top, axis=1)


def load_shares(count, total, reach, lean, full):
    weights = [(1 << 20) // math.isqrt(rank ** lean) + 1 for rank in range(1, count + 1)]
    largest = reach if full else min(reach, max(-(-total // count), total * weights[0] // sum(weights)))
    least = 1 if total - largest >= count - 1 else 0
    holding, rest = [largest] + [least] * (count - 1), total - largest - least * (count - 1)
    while rest > 0:
        movable = [i for i in range(1, count) if holding[i] < largest] or [i for i in range(1, count) if holding[i] < reach]
        mass, budget = sum([weights[i] for i in movable]), rest
        for i in movable:
            more = min(reach - holding[i], max(1, budget * weights[i] // mass), rest)
            holding[i] = holding[i] + more
            rest = rest - more
    return np.array(holding)


def centred(stream_key, shape, width, most, split=(), held_as=jnp.bfloat16):
    values = width * jax.random.normal(stream_key, shape, jnp.float32)
    if split:
        values = values * shard_levels(stream_key, shape, split, -0.22, 0.18)
    return jnp.clip(values, -most, most).astype(held_as)


def noise_with(stream_key, dims, scale, limit, split, heavy, held_as=jnp.bfloat16):
    drawn = scale * jax.random.normal(stream_key, dims, jnp.float32)
    if split:
        drawn = drawn * shard_levels(stream_key, dims, split, -0.22, 0.18)
    return jnp.clip(raised(drawn, jax.random.fold_in(stream_key, 3), *heavy), -limit, limit).astype(held_as)


def setup_inputs(seed: int = 0) -> dict:
    splits = jax.random.split(jax.random.key(seed), 14)
    residual_in = noise_with(splits[0], (TOKENS, MODEL_WIDTH), 1.0, 6.0, ((0, 32),), (0, 1, 32, 2.75))
    norm1_gain = jnp.clip(1.0 + 0.15 * jax.random.normal(splits[1], (MODEL_WIDTH,), jnp.float32), 0.25, 1.75)
    w_query = centred(splits[2], (MODEL_WIDTH, QUERY_HEADS * HEAD_SIZE), MODEL_WIDTH ** -0.5, 0.1875, ((0, 8), (1, 4)))
    key_weight = centred(splits[3], (MODEL_WIDTH, KEY_VALUE_HEADS * HEAD_SIZE), MODEL_WIDTH ** -0.5, 0.1875, ((0, 8), (1, 4)))
    value_weight = centred(splits[4], (MODEL_WIDTH, KEY_VALUE_HEADS * HEAD_SIZE), MODEL_WIDTH ** -0.5, 0.1875, ((0, 8), (1, 4)))
    w_out = centred(splits[5], (MODEL_WIDTH, QUERY_HEADS * HEAD_SIZE), (QUERY_HEADS * HEAD_SIZE // 8) ** -0.5, 0.5, ((0, 8), (1, 4)))
    norm2_gain = jnp.clip(1.0 + 0.15 * jax.random.normal(splits[6], (MODEL_WIDTH,), jnp.float32), 0.25, 1.75)
    w_gate = centred(splits[7], (E, MODEL_WIDTH, FF), MODEL_WIDTH ** -0.5, 0.1875, ((1, 8), (2, 4)))
    w_up = centred(splits[8], (E, MODEL_WIDTH, FF), MODEL_WIDTH ** -0.5, 0.1875, ((1, 8), (2, 4)))
    w_down = centred(splits[9], (E, MODEL_WIDTH, FF), (FF // 8) ** -0.5, 0.75, ((1, 8), (2, 4)))
    expert_ids_keys = jax.random.split(jax.random.fold_in(splits[10], 1), TOKENS // GT)
    expert_ids_turns = jax.random.permutation(jax.random.fold_in(splits[10], 3), TOKENS // GT)
    expert_ids = jax.vmap(lambda own, number: routed_block(jax.random.fold_in(splits[10], 2), own, number, GT, E, TOP, CAP, 0))(expert_ids_keys, expert_ids_turns).reshape((TOKENS, TOP))
    gate_weights = jnp.clip(jnp.exp(math.log(0.25) - 1.4271164 * jax.random.uniform(splits[11], (TOKENS, TOP), jnp.float32) ** shard_levels(splits[11], (TOKENS, TOP), ((0, 8),), -0.2, 0.2)), 0.06, 0.25)
    out_grad = noise_with(splits[12], (TOKENS, MODEL_WIDTH), 1.0, 6.0, ((0, 32),), (0, 1, 32, 2.75))
    return dict(residual_in=residual_in, norm1_gain=norm1_gain, w_query=w_query, key_weight=key_weight, value_weight=value_weight, w_out=w_out, norm2_gain=norm2_gain, w_gate=w_gate, w_up=w_up, w_down=w_down, expert_ids=expert_ids, gate_weights=gate_weights, out_grad=out_grad)


@jax.custom_vjp
def low(v):
    return lax.optimization_barrier(v.astype(jnp.bfloat16)).astype(jnp.float32)

@jax.custom_vjp
def low_back(v):
    return v

def low_keep(v):
    return (low(v), None)

def low_pass(kept, grad):
    return (grad,)

def back_keep(v):
    return (v, None)

def back_low(kept, grad):
    return (low(grad),)
low.defvjp(low_keep, low_pass)
low_back.defvjp(back_keep, back_low)
EPS = 1e-06
THETA = 10000.0
HIGH = lax.Precision.HIGHEST

def rope_tables(length, head_width):
    frequency = THETA ** (-(2.0 * jnp.arange(head_width // 2, dtype=jnp.float32)) / head_width)
    angles = jnp.arange(length, dtype=jnp.float32)[:, None] * frequency[None, :]
    return (jnp.cos(angles), jnp.sin(angles))

def apply_rotary(vector, cosine_table, sine_table):
    middle = vector.shape[-1] // 2
    leading = vector[..., :middle]
    trailing = vector[..., middle:]
    return jnp.concatenate([leading * cosine_table - trailing * sine_table, trailing * cosine_table + leading * sine_table], axis=-1)

def rms_norm(vector, gain_vec):
    factor = lax.rsqrt(lax.optimization_barrier(jnp.mean(vector * vector, axis=-1, keepdims=True)) + EPS)
    return vector * factor * gain_vec

def attend(pieces):
    query_seq, key_seq, value_seq = pieces
    repeat_factor = QUERY_HEADS // KEY_VALUE_HEADS
    key_all = jnp.repeat(key_seq, repeat_factor, axis=1)
    value_all = jnp.repeat(value_seq, repeat_factor, axis=1)
    scores = low_back(jnp.einsum('qhd,khd->hqk', query_seq, key_all, precision=HIGH) * HEAD_SIZE ** (-0.5))
    causal = jnp.arange(LEN)[:, None] >= jnp.arange(LEN)[None, :]
    scores = jnp.where(causal[None], scores, -1e+30)
    probs_low = low(jax.nn.softmax(scores, axis=-1))
    return jnp.einsum('hqk,khd->qhd', probs_low, value_all, precision=HIGH)

def block_layer(residual, params, route_rows, gate_rows):
    gain_one, weight_q, key_matrix, value_matrix, weight_o, gain_two, weight_g, weight_u, weight_d = params
    normed = low(rms_norm(residual, gain_one))
    cosine_table, sine_table = rope_tables(LEN, HEAD_SIZE)
    cosine_table = cosine_table[:, None, :]
    sine_table = sine_table[:, None, :]

    def split_into_heads(weight, count):
        return low_back(jnp.dot(normed, weight, precision=HIGH)).reshape(SEQ_GROUP, LEN, count, HEAD_SIZE)
    query = low(apply_rotary(split_into_heads(weight_q, QUERY_HEADS), cosine_table, sine_table))
    key_rows = low(apply_rotary(split_into_heads(key_matrix, KEY_VALUE_HEADS), cosine_table, sine_table))
    value_rows = low(split_into_heads(value_matrix, KEY_VALUE_HEADS))
    attended = lax.map(jax.checkpoint(attend), (query, key_rows, value_rows))
    heads_out = low(low_back(attended.reshape(GT, QUERY_HEADS * HEAD_SIZE)))
    middle = residual + low_back(jnp.dot(heads_out, weight_o.T, precision=HIGH))
    normed_two = low(rms_norm(middle, gain_two))
    flat = route_rows.reshape(-1)
    matches = (flat[:, None] == jnp.arange(E, dtype=jnp.int32)[None, :]).astype(jnp.int32)
    within = lax.optimization_barrier(jnp.sum((jnp.cumsum(matches, axis=0, dtype=jnp.int32) - 1) * matches, axis=1, dtype=jnp.int32))
    target = (flat * CAP + within).astype(jnp.int32)
    source = jnp.zeros((E * CAP,), jnp.int32).at[target].set(jnp.arange(GT * TOP, dtype=jnp.int32) // TOP)
    buffer = normed_two[source].reshape(E, CAP, MODEL_WIDTH)
    gate_proj = low_back(jnp.einsum('ecd,edf->ecf', buffer, weight_g, precision=HIGH))
    up_proj = low_back(jnp.einsum('ecd,edf->ecf', buffer, weight_u, precision=HIGH))
    hidden = low(jax.nn.silu(gate_proj) * up_proj)
    expert_out = low_back(jnp.einsum('ecf,edf->ecd', hidden, weight_d, precision=HIGH)).reshape(E * CAP, MODEL_WIDTH)
    picked = expert_out[target].reshape(GT, TOP, MODEL_WIDTH)
    return middle + lax.optimization_barrier(jnp.sum(picked * gate_rows[:, :, None], axis=1))

def reference(residual_in, norm1_gain, w_query, key_weight, value_weight, w_out, norm2_gain, w_gate, w_up, w_down, expert_ids, gate_weights, out_grad):
    params = tuple((weight.astype(jnp.float32) for weight in (norm1_gain, w_query, key_weight, value_weight, w_out, norm2_gain, w_gate, w_up, w_down)))
    inputs_all = (residual_in.astype(jnp.float32).reshape(N_DP, GT, MODEL_WIDTH), expert_ids.reshape(N_DP, GT, TOP), gate_weights.reshape(N_DP, GT, TOP), out_grad.astype(jnp.float32).reshape(N_DP, GT, MODEL_WIDTH))

    def group_step(totals, pieces):
        residual, route_rows, gate_rows, cotangent = pieces

        def forward(residual_f, param_f):
            return block_layer(residual_f, param_f, route_rows, gate_rows)
        result, pullback = jax.vjp(forward, residual, params)
        residual_grad, param_grads = pullback(cotangent)
        totals = tuple((accum + part for accum, part in zip(totals, param_grads)))
        return (totals, (result.astype(jnp.bfloat16), residual_grad))
    zero_init = tuple((jnp.zeros(weight.shape, jnp.float32) for weight in params))
    totals, (results, residual_grads) = lax.scan(group_step, zero_init, inputs_all)
    return (results.reshape(TOKENS, MODEL_WIDTH), residual_grads.reshape(TOKENS, MODEL_WIDTH), totals[0], totals[1], totals[2], totals[3], totals[4], totals[5], totals[6], totals[7], totals[8])
```

```python
import jax
import jax.numpy as jnp
from jax import lax
from jax.sharding import PartitionSpec as P

MODEL_WIDTH = 1024
HEAD_SIZE = 64
TOP = 8
LEN = 512
CAP = 288


EPS = 1e-06
THETA = 10000.0


def rope_tables(length, head_width):
    frequency = THETA ** (-(2.0 * jnp.arange(head_width // 2, dtype=jnp.float32)) / head_width)
    angles = jnp.arange(length, dtype=jnp.float32)[:, None] * frequency[None, :]
    return (jnp.cos(angles), jnp.sin(angles))


def apply_rotary(vector, cosine_table, sine_table):
    middle = vector.shape[-1] // 2
    leading = vector[..., :middle]
    trailing = vector[..., middle:]
    return jnp.concatenate(
        [
            leading * cosine_table - trailing * sine_table,
            trailing * cosine_table + leading * sine_table,
        ],
        axis=-1,
    )


def rotate_back(vector, cosine_table, sine_table):
    middle = vector.shape[-1] // 2
    leading = vector[..., :middle]
    trailing = vector[..., middle:]
    return jnp.concatenate(
        [
            leading * cosine_table + trailing * sine_table,
            trailing * cosine_table - leading * sine_table,
        ],
        axis=-1,
    )


def rms_factor(vector):
    return lax.rsqrt(jnp.mean(vector * vector, axis=-1, keepdims=True) + EPS)


def norm_back(vector, factor, gain_vec, grad_in):
    tilted = grad_in * gain_vec
    gain_part = jnp.sum(grad_in * vector * factor, axis=0)
    cubed = factor * factor * factor
    back = factor * tilted - vector * cubed * jnp.mean(tilted * vector, axis=-1, keepdims=True)
    return (back, gain_part)


BF = jnp.bfloat16
F32 = jnp.float32
REL = (0, 2, 4, 6, 1, 3, 5, 7)


def swap(value, axis, bit):
    size = lax.axis_size(axis)
    return lax.ppermute(value, axis, [(i, i ^ bit) for i in range(size)])


def mm(left, right):
    return jnp.dot(left, right, preferred_element_type=F32)


def mm_t(left, right):
    return lax.dot_general(left, right, (((1,), (1,)), ((), ())), preferred_element_type=F32)


def t_mm(left, right):
    return lax.dot_general(left, right, (((0,), (0,)), ((), ())), preferred_element_type=F32)


def to_relative(value):
    me = lax.axis_index("dp")
    return jnp.concatenate(
        [lax.dynamic_slice_in_dim(value, (me ^ r) * 128, 128, -1) for r in REL], axis=-1
    )


def from_relative(value):
    me = lax.axis_index("dp")
    pieces = []
    for block in range(8):
        s = me ^ block
        place = (s & 1) * 4 + ((s >> 2) & 1) * 2 + ((s >> 1) & 1)
        pieces.append(lax.dynamic_slice_in_dim(value, place * 128, 128, -1))
    return jnp.concatenate(pieces, axis=-1)


def gather_rows(shards):
    ways = [(2, 4) if i % 2 == 0 else (4, 2) for i in range(len(shards))]
    if lax.axis_size("dp") != 8:
        return [lax.all_gather(s, "dp", axis=0, tiled=True) for s in shards]
    first = [swap(s, "dp", w[0]) for s, w in zip(shards, ways)]
    pairs = [jnp.stack([s, f]) for s, f in zip(shards, first)]
    second = [swap(p, "dp", w[1]) for p, w in zip(pairs, ways)]
    quads = [
        jnp.stack([p, s], axis=0 if w[1] == 4 else 1) for p, s, w in zip(pairs, second, ways)
    ]
    third = [swap(q, "dp", 1) for q in quads]
    return [
        jnp.concatenate([q, t]).reshape(-1, q.shape[-1]) for q, t in zip(quads, third)
    ]


def add_low(a, b):
    return (a.astype(F32) + b.astype(F32)).astype(BF)


def scatter_rows(full, way):
    if lax.axis_size("dp") != 8:
        return lax.psum_scatter(full, "dp", scatter_dimension=0, tiled=True).astype(F32)
    columns = full.shape[1]
    quads = full.reshape(2, 2, 2, 128, columns)
    other = swap(quads[1], "dp", 1)
    held = add_low(quads[0], other)
    if way == 0:
        pair = add_low(held[:, 0], swap(held[:, 1], "dp", 2))
        last = swap(pair[1], "dp", 4)
    else:
        pair = add_low(held[0], swap(held[1], "dp", 4))
        last = swap(pair[1], "dp", 2)
    return pair[0].astype(F32) + last.astype(F32)


def total(value):
    for axis in ("dp", "tensor"):
        bit = 1
        while bit < lax.axis_size(axis):
            value = value + swap(value, axis, bit)
            bit *= 2
    return value


def gather_tokens(rows):
    me = lax.axis_index("tensor")
    size = lax.axis_size("tensor")
    held = jnp.stack([rows] + [swap(rows, "tensor", r) for r in range(1, size)])
    return jnp.concatenate(
        [lax.dynamic_index_in_dim(held, me ^ b, 0, keepdims=False) for b in range(size)]
    )


def scatter_tokens(full):
    me = lax.axis_index("tensor")
    size = lax.axis_size("tensor")
    blocks = full.reshape(size, -1, full.shape[-1])
    out = lax.dynamic_index_in_dim(blocks, me, 0, keepdims=False).astype(F32)
    for r in range(1, size):
        piece = lax.dynamic_index_in_dim(blocks, me ^ r, 0, keepdims=False)
        out = out + swap(piece, "tensor", r).astype(F32)
    return out


def rows_first(weight):
    return jnp.swapaxes(weight, 0, 1).reshape(weight.shape[1], -1)


def experts_first(grad, experts):
    return jnp.swapaxes(grad.reshape(grad.shape[0], experts, -1), 0, 1)


def local(
    residual_in,
    norm1_gain,
    w_query,
    key_weight,
    value_weight,
    w_out,
    norm2_gain,
    w_gate,
    w_up,
    w_down,
    expert_ids,
    gate_weights,
    out_grad,
):
    group_rows = expert_ids.shape[0]
    sequences = group_rows // LEN
    heads_q = w_query.shape[1] // HEAD_SIZE
    heads_kv = key_weight.shape[1] // HEAD_SIZE
    per_kv = heads_q // heads_kv
    experts = w_gate.shape[0]
    factor_s = HEAD_SIZE ** (-0.5)
    bf_type = jnp.bfloat16
    f_type = jnp.float32
    relative = lax.axis_size("dp") == 8
    order = to_relative if relative else (lambda v: v)
    unorder = from_relative if relative else (lambda v: v)
    q_width, k_width = w_query.shape[1], key_weight.shape[1]
    residual = order(residual_in).astype(f_type)
    gain_one, gain_two = order(norm1_gain), order(norm2_gain)
    cotangent = order(out_grad)
    full_qk, full_vo = gather_rows(
        [
            jnp.concatenate([w_query, key_weight], axis=1),
            jnp.concatenate([value_weight, w_out], axis=1),
        ]
    )
    full_v, full_o = full_vo[:, :k_width], full_vo[:, k_width:]
    factor_one = rms_factor(residual)
    normed = lax.all_gather(
        (residual * factor_one * gain_one).astype(bf_type), "tensor", axis=0, tiled=True
    )
    half = experts // 2
    shards = []
    for part in (slice(0, half), slice(half, None)):
        shards.append(
            jnp.concatenate([rows_first(w_gate[part]), rows_first(w_up[part])], axis=1)
        )
    for part in (slice(0, half), slice(half, None)):
        shards.append(rows_first(w_down[part]))
    shards, full_qk = lax.optimization_barrier((shards, full_qk))
    gu_a, gu_b, d_a, d_b = gather_rows(shards)
    grad_rows = gather_tokens(cotangent)
    cosine_table, sine_table = rope_tables(LEN, HEAD_SIZE)
    cosine_table = cosine_table[:, None, :]
    sine_table = sine_table[:, None, :]
    qk_raw = mm(normed, full_qk)
    query_raw = qk_raw[:, :q_width].reshape(sequences, LEN, heads_q, HEAD_SIZE)
    query = apply_rotary(query_raw, cosine_table, sine_table).astype(bf_type)
    keys_raw = qk_raw[:, q_width:].reshape(sequences, LEN, heads_kv, HEAD_SIZE)
    key_rows = apply_rotary(keys_raw, cosine_table, sine_table).astype(bf_type)
    value_rows = mm(normed, full_v).astype(bf_type).reshape(sequences, LEN, heads_kv, HEAD_SIZE)
    causal = jnp.arange(LEN)[:, None] >= jnp.arange(LEN)[None, :]

    def score_block(query_seq, key_seq):
        grouped = query_seq.reshape(LEN, heads_kv, per_kv, HEAD_SIZE)
        scores = (
            jnp.einsum("qkgd,skd->kgqs", grouped, key_seq, preferred_element_type=f_type) * factor_s
        )
        return jnp.where(causal, scores, -1e30)

    def forward_one(pieces):
        query_seq, key_seq, value_seq = pieces
        scores = score_block(query_seq, key_seq)
        row_max = jnp.max(scores, axis=-1, keepdims=True)
        exp_scores = jnp.exp(scores - row_max)
        row_sum = jnp.sum(exp_scores, axis=-1, keepdims=True)
        chances = (exp_scores / row_sum).astype(bf_type)
        attended = jnp.einsum("kgqs,skd->qkgd", chances, value_seq, preferred_element_type=f_type)
        return (attended.reshape(LEN, heads_q * HEAD_SIZE), (row_max + jnp.log(row_sum))[..., 0])

    attended, log_sums = lax.map(forward_one, (query, key_rows, value_rows))
    heads_out = attended.reshape(group_rows, heads_q * HEAD_SIZE).astype(bf_type)
    middle = residual + lax.psum_scatter(
        mm_t(heads_out, full_o).astype(bf_type), "tensor", scatter_dimension=0, tiled=True
    ).astype(f_type)
    factor_two = rms_factor(middle)
    normed_two = lax.all_gather(
        (middle * factor_two * gain_two).astype(bf_type), "tensor", axis=0, tiled=True
    )
    chosen = expert_ids[:, :, None] == jnp.arange(experts, dtype=jnp.int32)[None, None, :]
    mixing = jnp.sum(jnp.where(chosen, gate_weights[:, :, None], 0.0), axis=1)
    mixed_part, normed_two_part, low_grads = 0.0, 0.0, []
    for mix, gu, down in ((mixing[:, :half], gu_a, d_a), (mixing[:, half:], gu_b, d_b)):
        width = down.shape[1]
        spread = jnp.broadcast_to(
            mix[:, :, None], (group_rows, half, width // half)
        ).reshape(group_rows, width)
        both = mm(normed_two, gu)
        gate_proj, up_proj = both[:, :width], both[:, width:]
        sigmoid_g = jax.nn.sigmoid(gate_proj)
        activated = gate_proj * sigmoid_g
        hidden = (activated * up_proj * spread).astype(bf_type)
        hidden_grad = mm(grad_rows, down) * spread
        gate_grad = hidden_grad * up_proj * sigmoid_g * (1.0 + gate_proj * (1.0 - sigmoid_g))
        up_grad = hidden_grad * activated
        both_grad = jnp.concatenate([gate_grad.astype(bf_type), up_grad.astype(bf_type)], axis=1)
        normed_two_part = normed_two_part + mm_t(both_grad, gu)
        mixed_part = mixed_part + mm_t(hidden, down)
        low_grads.append((both_grad, hidden))
    normed_two_grad = lax.psum_scatter(
        normed_two_part.astype(bf_type), "tensor", scatter_dimension=0, tiled=True
    ).astype(f_type)
    residual_out = unorder((middle + scatter_tokens(mixed_part.astype(bf_type))).astype(bf_type))
    gu_grads, down_grads = [], []
    for way, (both_grad, hidden) in enumerate(low_grads):
        gu_grads.append(scatter_rows(t_mm(normed_two, both_grad).astype(bf_type), way))
        down_grads.append(scatter_rows(t_mm(grad_rows, hidden).astype(bf_type), way))
    width = down_grads[0].shape[1]
    w_gate_grad = jnp.concatenate([experts_first(g[:, :width], half) for g in gu_grads])
    w_up_grad = jnp.concatenate([experts_first(g[:, width:], half) for g in gu_grads])
    w_down_grad = jnp.concatenate([experts_first(g, half) for g in down_grads])
    back_two, gain_two_part = norm_back(middle, factor_two, gain_two, normed_two_grad)
    middle_grad = cotangent.astype(f_type) + back_two
    middle_rows = lax.all_gather(middle_grad.astype(bf_type), "tensor", axis=0, tiled=True)
    grad_out_w = t_mm(middle_rows, heads_out)
    heads_grad = jnp.dot(middle_rows, full_o, preferred_element_type=f_type).astype(bf_type)
    heads_grad = heads_grad.reshape(sequences, LEN, heads_q * HEAD_SIZE)

    def backward_one(pieces):
        query_seq, key_seq, value_seq, log_seq, grad_seq = pieces
        scores = score_block(query_seq, key_seq)
        chances = jnp.exp(scores - log_seq[..., None])
        grad_grouped = grad_seq.reshape(LEN, heads_kv, per_kv, HEAD_SIZE)
        grad_value = jnp.einsum(
            "kgqs,qkgd->skd", chances.astype(bf_type), grad_grouped, preferred_element_type=f_type
        )
        grad_chances = jnp.einsum(
            "qkgd,skd->kgqs", grad_grouped, value_seq, preferred_element_type=f_type
        )
        grad_scores = (
            chances * (grad_chances - jnp.sum(grad_chances * chances, axis=-1, keepdims=True))
        ).astype(bf_type)
        grad_query = (
            jnp.einsum("kgqs,skd->qkgd", grad_scores, key_seq, preferred_element_type=f_type)
            * factor_s
        )
        grouped = query_seq.reshape(LEN, heads_kv, per_kv, HEAD_SIZE)
        grad_key = (
            jnp.einsum("kgqs,qkgd->skd", grad_scores, grouped, preferred_element_type=f_type)
            * factor_s
        )
        return (grad_query.reshape(LEN, heads_q, HEAD_SIZE), grad_key, grad_value)

    query_rgrad, keys_rgrad, values_rgrad = lax.map(
        backward_one, (query, key_rows, value_rows, log_sums, heads_grad)
    )
    query_grad = (
        rotate_back(query_rgrad, cosine_table, sine_table)
        .astype(bf_type)
        .reshape(group_rows, heads_q * HEAD_SIZE)
    )
    keys_grad = (
        rotate_back(keys_rgrad, cosine_table, sine_table)
        .astype(bf_type)
        .reshape(group_rows, heads_kv * HEAD_SIZE)
    )
    values_grad = values_rgrad.astype(bf_type).reshape(group_rows, heads_kv * HEAD_SIZE)
    qk_grad = jnp.concatenate([query_grad, keys_grad], axis=1)
    grad_qk_w = scatter_rows(t_mm(normed, qk_grad).astype(bf_type), 0)
    grad_vo_w = scatter_rows(
        jnp.concatenate([t_mm(normed, values_grad), grad_out_w], axis=1).astype(bf_type), 1
    )
    w_query_grad, w_key_grad = grad_qk_w[:, :q_width], grad_qk_w[:, q_width:]
    w_value_grad, w_out_grad = grad_vo_w[:, :k_width], grad_vo_w[:, k_width:]
    normed_part = mm_t(qk_grad, full_qk) + mm_t(values_grad, full_v)
    gain_one_part = jnp.sum(normed_part * normed.astype(f_type), axis=0) / gain_one
    normed_grad = lax.psum_scatter(
        normed_part.astype(bf_type), "tensor", scatter_dimension=0, tiled=True
    ).astype(f_type)
    back_one, _ = norm_back(residual, factor_one, gain_one, normed_grad)
    input_grad = unorder(middle_grad + back_one)
    gains = total(unorder(jnp.stack([gain_one_part, gain_two_part])))
    norm1_gain_grad, norm2_gain_grad = gains[0], gains[1]
    return (
        residual_out,
        input_grad,
        norm1_gain_grad,
        w_query_grad,
        w_key_grad,
        w_value_grad,
        w_out_grad,
        norm2_gain_grad,
        w_gate_grad,
        w_up_grad,
        w_down_grad,
    )


def solution(mesh):
    placed = (
        P(("dp", "tensor"), None),
        P(),
        P("dp", "tensor"),
        P("dp", "tensor"),
        P("dp", "tensor"),
        P("dp", "tensor"),
        P(),
        P(None, "dp", "tensor"),
        P(None, "dp", "tensor"),
        P(None, "dp", "tensor"),
        P("dp", None),
        P("dp", None),
        P(("dp", "tensor"), None),
    )
    return jax.shard_map(
        local,
        mesh=mesh,
        in_specs=placed,
        out_specs=(
            P(("dp", "tensor"), None),
            P(("dp", "tensor"), None),
            P(),
            P("dp", "tensor"),
            P("dp", "tensor"),
            P("dp", "tensor"),
            P("dp", "tensor"),
            P(),
            P(None, "dp", "tensor"),
            P(None, "dp", "tensor"),
            P(None, "dp", "tensor"),
        ),
        check_vma=False,
    )
```

```python
import functools

import jax
import jax.numpy as jnp
from jax import lax
from jax.experimental import pallas as pl
from jax.experimental.pallas import tpu as pltpu
from jax.sharding import PartitionSpec as P

MODEL_WIDTH = 1024
HEAD_SIZE = 64
TOP = 8
LEN = 512
CAP = 288


EPS = 1e-06
THETA = 10000.0


def rope_tables(length, head_width):
    frequency = THETA ** (-(2.0 * jnp.arange(head_width // 2, dtype=jnp.float32)) / head_width)
    angles = jnp.arange(length, dtype=jnp.float32)[:, None] * frequency[None, :]
    return (jnp.cos(angles), jnp.sin(angles))


def apply_rotary(vector, cosine_table, sine_table):
    middle = vector.shape[-1] // 2
    leading = vector[..., :middle]
    trailing = vector[..., middle:]
    return jnp.concatenate(
        [
            leading * cosine_table - trailing * sine_table,
            trailing * cosine_table + leading * sine_table,
        ],
        axis=-1,
    )


def rotate_back(vector, cosine_table, sine_table):
    middle = vector.shape[-1] // 2
    leading = vector[..., :middle]
    trailing = vector[..., middle:]
    return jnp.concatenate(
        [
            leading * cosine_table + trailing * sine_table,
            trailing * cosine_table - leading * sine_table,
        ],
        axis=-1,
    )


def rms_factor(vector):
    return lax.rsqrt(jnp.mean(vector * vector, axis=-1, keepdims=True) + EPS)


def norm_back(vector, factor, gain_vec, grad_in):
    tilted = grad_in * gain_vec
    gain_part = jnp.sum(grad_in * vector * factor, axis=0)
    cubed = factor * factor * factor
    back = factor * tilted - vector * cubed * jnp.mean(tilted * vector, axis=-1, keepdims=True)
    return (back, gain_part)


BF = jnp.bfloat16
F32 = jnp.float32
REL = (0, 2, 4, 6, 1, 3, 5, 7)


def swap(value, axis, bit):
    size = lax.axis_size(axis)
    return lax.ppermute(value, axis, [(i, i ^ bit) for i in range(size)])


def mm(left, right):
    return jnp.dot(left, right, preferred_element_type=F32)


def mm_t(left, right):
    return lax.dot_general(left, right, (((1,), (1,)), ((), ())), preferred_element_type=F32)


def t_mm(left, right):
    return lax.dot_general(left, right, (((0,), (0,)), ((), ())), preferred_element_type=F32)


def reorder_kernel(inverse, *refs):
    count = len(refs) // 2
    me = lax.axis_index("dp")
    for p in range(8):
        if inverse:
            s = jnp.bitwise_xor(me, p)
            block = (s % 2) * 4 + ((s // 4) % 2) * 2 + (s // 2) % 2
        else:
            block = jnp.bitwise_xor(me, REL[p])
        start = pl.multiple_of(block * 128, 128)
        for taken, given in zip(refs[:count], refs[count:]):
            given[:, p * 128 : (p + 1) * 128] = taken[:, pl.ds(start, 128)]


def reorder(values, inverse):
    if lax.axis_size("dp") != 8:
        return values
    return pl.pallas_call(
        functools.partial(reorder_kernel, inverse),
        out_shape=[jax.ShapeDtypeStruct(v.shape, v.dtype) for v in values],
        in_specs=[pl.BlockSpec(memory_space=pltpu.VMEM)] * len(values),
        out_specs=[pl.BlockSpec(memory_space=pltpu.VMEM)] * len(values),
    )(*values)


def experts_kernel(
    way, x, dy, spread, pair, second, pair_o, second_o, n2, mixed, hg, gg, ug, wg, wu, wd
):
    pieces = (pair, second, pair_o, second_o)
    for core in range(2):
        for late in range(2):
            for j in range(2):
                place = core * 4 + (late * 2 + j if way == 0 else j * 2 + late)
                rows = slice(place * 128, (place + 1) * 128)
                for k, weight in enumerate((wg, wu, wd)):
                    for e in range(2):
                        weight[rows, e * 128 : (e + 1) * 128] = pieces[core * 2 + late][j, k, e]
    gate_proj = mm(x[...], wg[...])
    up_proj = mm(x[...], wu[...])
    hidden_grad = mm(dy[...], wd[...]) * spread[...]
    sigmoid_g = 1.0 / (1.0 + jnp.exp(-gate_proj))
    activated = gate_proj * sigmoid_g
    hidden = (activated * up_proj * spread[...]).astype(BF)
    gate_grad = (
        hidden_grad * up_proj * sigmoid_g * (1.0 + gate_proj * (1.0 - sigmoid_g))
    ).astype(BF)
    up_grad = (hidden_grad * activated).astype(BF)
    hg[...] = hidden
    gg[...] = gate_grad
    ug[...] = up_grad
    n2_step = mm_t(gate_grad, wg[...]) + mm_t(up_grad, wu[...])
    mixed_step = mm_t(hidden, wd[...])

    @pl.when(pl.program_id(0) == 0)
    def _():
        n2[...] = n2_step
        mixed[...] = mixed_step

    @pl.when(pl.program_id(0) != 0)
    def _():
        n2[...] += n2_step
        mixed[...] += mixed_step


def experts_part(way, x, dy, spread, pieces):
    rows, width = x.shape
    half = pieces[0].shape[2]
    whole = pl.BlockSpec((rows, width), lambda i: (0, 0))
    tile = pl.BlockSpec((rows, 256), lambda i: (0, i))
    piece = pl.BlockSpec((2, 3, 2, 128, 128), lambda i: (0, 0, i, 0, 0))
    hidden_shape = jax.ShapeDtypeStruct((rows, half * 128), BF)
    return pl.pallas_call(
        functools.partial(experts_kernel, way),
        grid=(half // 2,),
        in_specs=[whole, whole, tile, piece, piece, piece, piece],
        out_specs=[whole, whole, tile, tile, tile],
        out_shape=[jax.ShapeDtypeStruct((rows, width), F32)] * 2 + [hidden_shape] * 3,
        scratch_shapes=[pltpu.VMEM((width, 256), BF)] * 3,
        compiler_params=pltpu.CompilerParams(vmem_limit_bytes=50 * 2**20),
        cost_estimate=pl.CostEstimate(
            flops=12 * rows * width * half * 128, bytes_accessed=16 * 2**20, transcendentals=0
        ),
    )(x, dy, spread, *pieces)


def weight_grads_kernel(way, x_t, dy_t, hg, gg, ug, sent, kept):
    for k, (left, right) in enumerate(((x_t, gg), (x_t, ug), (dy_t, hg))):
        grad = mm(left[...], right[...]).astype(BF)
        for core in range(2):
            for y in range(2):
                for x in range(2):
                    place = core * 4 + y * 2 + x
                    slot = (1 - x) * 2 + 1 - y if way == 0 else (1 - y) * 2 + 1 - x
                    for e in range(2):
                        (sent if core else kept)[slot, k, e] = grad[
                            place * 128 : (place + 1) * 128, e * 128 : (e + 1) * 128
                        ]


def weight_grads(way, x_t, dy_t, hg, gg, ug):
    width, rows = x_t.shape
    half = hg.shape[1] // 128
    whole = pl.BlockSpec((width, rows), lambda i: (0, 0))
    tile = pl.BlockSpec((rows, 256), lambda i: (0, i))
    quad = pl.BlockSpec((4, 3, 2, 128, 128), lambda i: (0, 0, i, 0, 0))
    return pl.pallas_call(
        functools.partial(weight_grads_kernel, way),
        grid=(half // 2,),
        in_specs=[whole, whole, tile, tile, tile],
        out_specs=[quad, quad],
        out_shape=[jax.ShapeDtypeStruct((4, 3, half, 128, 128), BF)] * 2,
        compiler_params=pltpu.CompilerParams(vmem_limit_bytes=50 * 2**20),
        cost_estimate=pl.CostEstimate(
            flops=6 * rows * width * half * 128, bytes_accessed=10 * 2**20, transcendentals=0
        ),
    )(x_t, dy_t, hg, gg, ug)


WAYS = ((2, 4), (4, 2))


def sum_pieces(way, sent, kept):
    near, far = WAYS[way]
    core = swap(sent, "dp", 1)
    first = swap(add_low(kept[:2], core[:2]), "dp", near)
    held = kept[2:].astype(F32) + core[2:].astype(F32) + first.astype(F32)
    return held[1] + swap(held[0].astype(BF), "dp", far).astype(F32)


def gather_rows(shards):
    ways = [(2, 4) if i % 2 == 0 else (4, 2) for i in range(len(shards))]
    if lax.axis_size("dp") != 8:
        return [lax.all_gather(s, "dp", axis=0, tiled=True) for s in shards]
    first = [swap(s, "dp", w[0]) for s, w in zip(shards, ways)]
    pairs = [jnp.stack([s, f]) for s, f in zip(shards, first)]
    second = [swap(p, "dp", w[1]) for p, w in zip(pairs, ways)]
    quads = [
        jnp.stack([p, s], axis=0 if w[1] == 4 else 1) for p, s, w in zip(pairs, second, ways)
    ]
    third = [swap(q, "dp", 1) for q in quads]
    return [
        jnp.concatenate([q, t]).reshape(-1, q.shape[-1]) for q, t in zip(quads, third)
    ]


def add_low(a, b):
    return (a.astype(F32) + b.astype(F32)).astype(BF)


def scatter_rows(full, way):
    if lax.axis_size("dp") != 8:
        return lax.psum_scatter(full, "dp", scatter_dimension=0, tiled=True).astype(F32)
    columns = full.shape[1]
    quads = full.reshape(2, 2, 2, 128, columns)
    other = swap(quads[1], "dp", 1)
    held = add_low(quads[0], other)
    if way == 0:
        pair = add_low(held[:, 0], swap(held[:, 1], "dp", 2))
        last = swap(pair[1], "dp", 4)
    else:
        pair = add_low(held[0], swap(held[1], "dp", 4))
        last = swap(pair[1], "dp", 2)
    return pair[0].astype(F32) + last.astype(F32)


def total(value):
    for axis in ("dp", "tensor"):
        bit = 1
        while bit < lax.axis_size(axis):
            value = value + swap(value, axis, bit)
            bit *= 2
    return value


def gather_tokens(rows):
    me = lax.axis_index("tensor")
    size = lax.axis_size("tensor")
    held = jnp.stack([rows] + [swap(rows, "tensor", r) for r in range(1, size)])
    return jnp.concatenate(
        [lax.dynamic_index_in_dim(held, me ^ b, 0, keepdims=False) for b in range(size)]
    )


def scatter_tokens(full):
    me = lax.axis_index("tensor")
    size = lax.axis_size("tensor")
    blocks = full.reshape(size, -1, full.shape[-1])
    out = lax.dynamic_index_in_dim(blocks, me, 0, keepdims=False).astype(F32)
    for r in range(1, size):
        piece = lax.dynamic_index_in_dim(blocks, me ^ r, 0, keepdims=False)
        out = out + swap(piece, "tensor", r).astype(F32)
    return out


def rows_first(weight):
    return jnp.swapaxes(weight, 0, 1).reshape(weight.shape[1], -1)


def experts_first(grad, experts):
    return jnp.swapaxes(grad.reshape(grad.shape[0], experts, -1), 0, 1)


def local(
    residual_in,
    norm1_gain,
    w_query,
    key_weight,
    value_weight,
    w_out,
    norm2_gain,
    w_gate,
    w_up,
    w_down,
    expert_ids,
    gate_weights,
    out_grad,
):
    group_rows = expert_ids.shape[0]
    sequences = group_rows // LEN
    heads_q = w_query.shape[1] // HEAD_SIZE
    heads_kv = key_weight.shape[1] // HEAD_SIZE
    per_kv = heads_q // heads_kv
    experts = w_gate.shape[0]
    factor_s = HEAD_SIZE ** (-0.5)
    bf_type = jnp.bfloat16
    f_type = jnp.float32
    relative = lax.axis_size("dp") == 8
    q_width, k_width = w_query.shape[1], key_weight.shape[1]
    residual, cotangent, gain_one, gain_two = reorder(
        (residual_in, out_grad, norm1_gain[None, :], norm2_gain[None, :]), False
    )
    residual = residual.astype(f_type)
    gain_one, gain_two = gain_one[0], gain_two[0]
    full_qk, full_vo = gather_rows(
        [
            jnp.concatenate([w_query, key_weight], axis=1),
            jnp.concatenate([value_weight, w_out], axis=1),
        ]
    )
    full_v, full_o = full_vo[:, :k_width], full_vo[:, k_width:]
    factor_one = rms_factor(residual)
    normed = lax.all_gather(
        (residual * factor_one * gain_one).astype(bf_type), "tensor", axis=0, tiled=True
    )
    half = experts // 2
    parts = (slice(0, half), slice(half, None))
    if relative:
        shards = [jnp.stack([w_gate[p], w_up[p], w_down[p]]) for p in parts]
        shards, full_qk = lax.optimization_barrier((shards, full_qk))
        firsts = [swap(w, "dp", way[0]) for w, way in zip(shards, WAYS)]
        pairs = [jnp.stack([w, f]) for w, f in zip(shards, firsts)]
        seconds = [swap(p, "dp", way[1]) for p, way in zip(pairs, WAYS)]
    else:
        shards = [
            jnp.concatenate([rows_first(w_gate[p]), rows_first(w_up[p])], axis=1) for p in parts
        ] + [rows_first(w_down[p]) for p in parts]
        shards, full_qk = lax.optimization_barrier((shards, full_qk))
        gu_a, gu_b, d_a, d_b = gather_rows(shards)
    grad_rows = gather_tokens(cotangent)
    cosine_table, sine_table = rope_tables(LEN, HEAD_SIZE)
    cosine_table = cosine_table[:, None, :]
    sine_table = sine_table[:, None, :]
    qk_raw = mm(normed, full_qk)
    query_raw = qk_raw[:, :q_width].reshape(sequences, LEN, heads_q, HEAD_SIZE)
    query = apply_rotary(query_raw, cosine_table, sine_table).astype(bf_type)
    keys_raw = qk_raw[:, q_width:].reshape(sequences, LEN, heads_kv, HEAD_SIZE)
    key_rows = apply_rotary(keys_raw, cosine_table, sine_table).astype(bf_type)
    value_rows = mm(normed, full_v).astype(bf_type).reshape(sequences, LEN, heads_kv, HEAD_SIZE)
    causal = jnp.arange(LEN)[:, None] >= jnp.arange(LEN)[None, :]

    def score_block(query_seq, key_seq):
        grouped = query_seq.reshape(LEN, heads_kv, per_kv, HEAD_SIZE)
        scores = (
            jnp.einsum("qkgd,skd->kgqs", grouped, key_seq, preferred_element_type=f_type) * factor_s
        )
        return jnp.where(causal, scores, -1e30)

    def forward_one(pieces):
        query_seq, key_seq, value_seq = pieces
        scores = score_block(query_seq, key_seq)
        row_max = jnp.max(scores, axis=-1, keepdims=True)
        exp_scores = jnp.exp(scores - row_max)
        row_sum = jnp.sum(exp_scores, axis=-1, keepdims=True)
        chances = (exp_scores / row_sum).astype(bf_type)
        attended = jnp.einsum("kgqs,skd->qkgd", chances, value_seq, preferred_element_type=f_type)
        return (attended.reshape(LEN, heads_q * HEAD_SIZE), (row_max + jnp.log(row_sum))[..., 0])

    attended, log_sums = lax.map(forward_one, (query, key_rows, value_rows))
    heads_out = attended.reshape(group_rows, heads_q * HEAD_SIZE).astype(bf_type)
    middle = residual + lax.psum_scatter(
        mm_t(heads_out, full_o).astype(bf_type), "tensor", scatter_dimension=0, tiled=True
    ).astype(f_type)
    factor_two = rms_factor(middle)
    normed_two_rows = (middle * factor_two * gain_two).astype(bf_type)
    normed_two = lax.all_gather(normed_two_rows, "tensor", axis=0, tiled=True)
    chosen = expert_ids[:, :, None] == jnp.arange(experts, dtype=jnp.int32)[None, None, :]
    mixing = jnp.sum(jnp.where(chosen, gate_weights[:, :, None], 0.0), axis=1)
    if relative:
        pairs, seconds, _ = lax.optimization_barrier((pairs, seconds, normed_two_rows))
        spread = jnp.broadcast_to(
            mixing[:, :, None], (group_rows, experts, 128)
        ).reshape(group_rows, experts * 128)
        results = []
        for way in range(2):
            pieces = (pairs[way], seconds[way], swap(pairs[way], "dp", 1))
            pieces = pieces + (swap(seconds[way], "dp", 1),)
            columns = spread[:, way * half * 128 : (way + 1) * half * 128]
            results.append(experts_part(way, normed_two, grad_rows, columns, pieces))
        normed_two_part = results[0][0] + results[1][0]
        mixed_part = results[0][1] + results[1][1]
    else:
        mixed_part, normed_two_part, low_grads = 0.0, 0.0, []
        for mix, gu, down in ((mixing[:, :half], gu_a, d_a), (mixing[:, half:], gu_b, d_b)):
            width = down.shape[1]
            spread = jnp.broadcast_to(
                mix[:, :, None], (group_rows, half, width // half)
            ).reshape(group_rows, width)
            both = mm(normed_two, gu)
            gate_proj, up_proj = both[:, :width], both[:, width:]
            sigmoid_g = jax.nn.sigmoid(gate_proj)
            activated = gate_proj * sigmoid_g
            hidden = (activated * up_proj * spread).astype(bf_type)
            hidden_grad = mm(grad_rows, down) * spread
            gate_grad = hidden_grad * up_proj * sigmoid_g * (1.0 + gate_proj * (1.0 - sigmoid_g))
            up_grad = hidden_grad * activated
            both_grad = jnp.concatenate([gate_grad.astype(bf_type), up_grad.astype(bf_type)], axis=1)
            normed_two_part = normed_two_part + mm_t(both_grad, gu)
            mixed_part = mixed_part + mm_t(hidden, down)
            low_grads.append((both_grad, hidden))
    normed_two_grad = lax.psum_scatter(
        normed_two_part.astype(bf_type), "tensor", scatter_dimension=0, tiled=True
    ).astype(f_type)
    residual_out = (middle + scatter_tokens(mixed_part.astype(bf_type))).astype(bf_type)
    if relative:
        x_t, dy_t = normed_two.T, grad_rows.T
        sums = []
        for way in range(2):
            sent, kept = weight_grads(way, x_t, dy_t, *results[way][2:])
            sums.append(sum_pieces(way, sent, kept))
        w_gate_grad, w_up_grad, w_down_grad = (
            jnp.concatenate([sums[0][k], sums[1][k]]) for k in range(3)
        )
    else:
        gu_grads, down_grads = [], []
        for way, (both_grad, hidden) in enumerate(low_grads):
            gu_grads.append(scatter_rows(t_mm(normed_two, both_grad).astype(bf_type), way))
            down_grads.append(scatter_rows(t_mm(grad_rows, hidden).astype(bf_type), way))
        width = down_grads[0].shape[1]
        w_gate_grad = jnp.concatenate([experts_first(g[:, :width], half) for g in gu_grads])
        w_up_grad = jnp.concatenate([experts_first(g[:, width:], half) for g in gu_grads])
        w_down_grad = jnp.concatenate([experts_first(g, half) for g in down_grads])
    back_two, gain_two_part = norm_back(middle, factor_two, gain_two, normed_two_grad)
    middle_grad = cotangent.astype(f_type) + back_two
    middle_rows = lax.all_gather(middle_grad.astype(bf_type), "tensor", axis=0, tiled=True)
    grad_out_w = t_mm(middle_rows, heads_out)
    heads_grad = jnp.dot(middle_rows, full_o, preferred_element_type=f_type).astype(bf_type)
    heads_grad = heads_grad.reshape(sequences, LEN, heads_q * HEAD_SIZE)

    def backward_one(pieces):
        query_seq, key_seq, value_seq, log_seq, grad_seq = pieces
        scores = score_block(query_seq, key_seq)
        chances = jnp.exp(scores - log_seq[..., None])
        grad_grouped = grad_seq.reshape(LEN, heads_kv, per_kv, HEAD_SIZE)
        grad_value = jnp.einsum(
            "kgqs,qkgd->skd", chances.astype(bf_type), grad_grouped, preferred_element_type=f_type
        )
        grad_chances = jnp.einsum(
            "qkgd,skd->kgqs", grad_grouped, value_seq, preferred_element_type=f_type
        )
        grad_scores = (
            chances * (grad_chances - jnp.sum(grad_chances * chances, axis=-1, keepdims=True))
        ).astype(bf_type)
        grad_query = (
            jnp.einsum("kgqs,skd->qkgd", grad_scores, key_seq, preferred_element_type=f_type)
            * factor_s
        )
        grouped = query_seq.reshape(LEN, heads_kv, per_kv, HEAD_SIZE)
        grad_key = (
            jnp.einsum("kgqs,qkgd->skd", grad_scores, grouped, preferred_element_type=f_type)
            * factor_s
        )
        return (grad_query.reshape(LEN, heads_q, HEAD_SIZE), grad_key, grad_value)

    query_rgrad, keys_rgrad, values_rgrad = lax.map(
        backward_one, (query, key_rows, value_rows, log_sums, heads_grad)
    )
    query_grad = (
        rotate_back(query_rgrad, cosine_table, sine_table)
        .astype(bf_type)
        .reshape(group_rows, heads_q * HEAD_SIZE)
    )
    keys_grad = (
        rotate_back(keys_rgrad, cosine_table, sine_table)
        .astype(bf_type)
        .reshape(group_rows, heads_kv * HEAD_SIZE)
    )
    values_grad = values_rgrad.astype(bf_type).reshape(group_rows, heads_kv * HEAD_SIZE)
    qk_grad = jnp.concatenate([query_grad, keys_grad], axis=1)
    grad_qk_w = scatter_rows(t_mm(normed, qk_grad).astype(bf_type), 0)
    grad_vo_w = scatter_rows(
        jnp.concatenate([t_mm(normed, values_grad), grad_out_w], axis=1).astype(bf_type), 1
    )
    w_query_grad, w_key_grad = grad_qk_w[:, :q_width], grad_qk_w[:, q_width:]
    w_value_grad, w_out_grad = grad_vo_w[:, :k_width], grad_vo_w[:, k_width:]
    normed_part = mm_t(qk_grad, full_qk) + mm_t(values_grad, full_v)
    gain_one_part = jnp.sum(normed_part * normed.astype(f_type), axis=0) / gain_one
    normed_grad = lax.psum_scatter(
        normed_part.astype(bf_type), "tensor", scatter_dimension=0, tiled=True
    ).astype(f_type)
    back_one, _ = norm_back(residual, factor_one, gain_one, normed_grad)
    gains = jnp.stack([gain_one_part, gain_two_part])
    residual_out, input_grad, gains = reorder(
        (residual_out, middle_grad + back_one, gains), True
    )
    gains = total(gains)
    norm1_gain_grad, norm2_gain_grad = gains[0], gains[1]
    return (
        residual_out,
        input_grad,
        norm1_gain_grad,
        w_query_grad,
        w_key_grad,
        w_value_grad,
        w_out_grad,
        norm2_gain_grad,
        w_gate_grad,
        w_up_grad,
        w_down_grad,
    )


def solution(mesh):
    placed = (
        P(("dp", "tensor"), None),
        P(),
        P("dp", "tensor"),
        P("dp", "tensor"),
        P("dp", "tensor"),
        P("dp", "tensor"),
        P(),
        P(None, "dp", "tensor"),
        P(None, "dp", "tensor"),
        P(None, "dp", "tensor"),
        P("dp", None),
        P("dp", None),
        P(("dp", "tensor"), None),
    )
    return jax.shard_map(
        local,
        mesh=mesh,
        in_specs=placed,
        out_specs=(
            P(("dp", "tensor"), None),
            P(("dp", "tensor"), None),
            P(),
            P("dp", "tensor"),
            P("dp", "tensor"),
            P("dp", "tensor"),
            P("dp", "tensor"),
            P(),
            P(None, "dp", "tensor"),
            P(None, "dp", "tensor"),
            P(None, "dp", "tensor"),
        ),
        check_vma=False,
    )
```

```python
import functools

import jax
import jax.numpy as jnp
from jax import lax
from jax.experimental import pallas as pl
from jax.experimental.pallas import tpu as pltpu
from jax.sharding import PartitionSpec as P

MODEL_WIDTH = 1024
HEAD_SIZE = 64
TOP = 8
LEN = 512
CAP = 288


EPS = 1e-06
THETA = 10000.0


def rope_tables(length, head_width):
    frequency = THETA ** (-(2.0 * jnp.arange(head_width // 2, dtype=jnp.float32)) / head_width)
    angles = jnp.arange(length, dtype=jnp.float32)[:, None] * frequency[None, :]
    return (jnp.cos(angles), jnp.sin(angles))


def apply_rotary(vector, cosine_table, sine_table):
    middle = vector.shape[-1] // 2
    leading = vector[..., :middle]
    trailing = vector[..., middle:]
    return jnp.concatenate(
        [
            leading * cosine_table - trailing * sine_table,
            trailing * cosine_table + leading * sine_table,
        ],
        axis=-1,
    )


def rotate_back(vector, cosine_table, sine_table):
    middle = vector.shape[-1] // 2
    leading = vector[..., :middle]
    trailing = vector[..., middle:]
    return jnp.concatenate(
        [
            leading * cosine_table + trailing * sine_table,
            trailing * cosine_table - leading * sine_table,
        ],
        axis=-1,
    )


def rms_factor(vector):
    return lax.rsqrt(jnp.mean(vector * vector, axis=-1, keepdims=True) + EPS)


def norm_back(vector, factor, gain_vec, grad_in):
    tilted = grad_in * gain_vec
    gain_part = jnp.sum(grad_in * vector * factor, axis=0)
    cubed = factor * factor * factor
    back = factor * tilted - vector * cubed * jnp.mean(tilted * vector, axis=-1, keepdims=True)
    return (back, gain_part)


BF = jnp.bfloat16
F32 = jnp.float32
REL = (0, 2, 4, 6, 1, 3, 5, 7)


def swap(value, axis, bit):
    size = lax.axis_size(axis)
    return lax.ppermute(value, axis, [(i, i ^ bit) for i in range(size)])


def mm(left, right):
    return jnp.dot(left, right, preferred_element_type=F32)


def mm_t(left, right):
    return lax.dot_general(left, right, (((1,), (1,)), ((), ())), preferred_element_type=F32)


def t_mm(left, right):
    return lax.dot_general(left, right, (((0,), (0,)), ((), ())), preferred_element_type=F32)


def reorder_kernel(inverse, *refs):
    count = len(refs) // 2
    me = lax.axis_index("dp")
    for p in range(8):
        if inverse:
            s = jnp.bitwise_xor(me, p)
            block = (s % 2) * 4 + ((s // 4) % 2) * 2 + (s // 2) % 2
        else:
            block = jnp.bitwise_xor(me, REL[p])
        start = pl.multiple_of(block * 128, 128)
        for taken, given in zip(refs[:count], refs[count:]):
            given[:, p * 128 : (p + 1) * 128] = taken[:, pl.ds(start, 128)]


def reorder(values, inverse):
    if lax.axis_size("dp") != 8:
        return values
    return pl.pallas_call(
        functools.partial(reorder_kernel, inverse),
        out_shape=[jax.ShapeDtypeStruct(v.shape, v.dtype) for v in values],
        in_specs=[pl.BlockSpec(memory_space=pltpu.VMEM)] * len(values),
        out_specs=[pl.BlockSpec(memory_space=pltpu.VMEM)] * len(values),
    )(*values)


def experts_kernel(
    way, x, dy, mixing, pair, second, pair_o, second_o, n2, mixed, hg, gg, ug, wg, wu, wd
):
    pieces = (pair, second, pair_o, second_o)
    for core in range(2):
        for late in range(2):
            for j in range(2):
                place = core * 4 + (late * 2 + j if way == 0 else j * 2 + late)
                rows = slice(place * 128, (place + 1) * 128)
                for k, weight in enumerate((wg, wu, wd)):
                    for e in range(2):
                        weight[rows, e * 128 : (e + 1) * 128] = pieces[core * 2 + late][j, k, e]
    step = pl.program_id(0)
    lanes = lax.broadcasted_iota(jnp.int32, mixing.shape, 1)
    taken = []
    for e in range(2):
        expert = way * 2 * pl.num_programs(0) + 2 * step + e
        column = jnp.sum(jnp.where(lanes == expert, mixing[...], 0.0), axis=1, keepdims=True)
        taken.append(jnp.broadcast_to(column, (column.shape[0], 128)))
    spread = jnp.concatenate(taken, axis=1)
    gate_proj = mm(x[...], wg[...])
    up_proj = mm(x[...], wu[...])
    hidden_grad = mm(dy[...], wd[...]) * spread
    sigmoid_g = 1.0 / (1.0 + jnp.exp(-gate_proj))
    activated = gate_proj * sigmoid_g
    hidden = (activated * up_proj * spread).astype(BF)
    gate_grad = (
        hidden_grad * up_proj * sigmoid_g * (1.0 + gate_proj * (1.0 - sigmoid_g))
    ).astype(BF)
    up_grad = (hidden_grad * activated).astype(BF)
    hg[...] = hidden
    gg[...] = gate_grad
    ug[...] = up_grad
    n2_step = mm_t(gate_grad, wg[...]) + mm_t(up_grad, wu[...])
    mixed_step = mm_t(hidden, wd[...])

    @pl.when(pl.program_id(0) == 0)
    def _():
        n2[...] = n2_step
        mixed[...] = mixed_step

    @pl.when(pl.program_id(0) != 0)
    def _():
        n2[...] += n2_step
        mixed[...] += mixed_step


def experts_part(way, x, dy, mixing, pieces):
    rows, width = x.shape
    half = pieces[0].shape[2]
    whole = pl.BlockSpec((rows, width), lambda i: (0, 0))
    tile = pl.BlockSpec((rows, 256), lambda i: (0, i))
    gates = pl.BlockSpec(mixing.shape, lambda i: (0, 0))
    piece = pl.BlockSpec((2, 3, 2, 128, 128), lambda i: (0, 0, i, 0, 0))
    hidden_shape = jax.ShapeDtypeStruct((rows, half * 128), BF)
    return pl.pallas_call(
        functools.partial(experts_kernel, way),
        grid=(half // 2,),
        in_specs=[whole, whole, gates, piece, piece, piece, piece],
        out_specs=[whole, whole, tile, tile, tile],
        out_shape=[jax.ShapeDtypeStruct((rows, width), F32)] * 2 + [hidden_shape] * 3,
        scratch_shapes=[pltpu.VMEM((width, 256), BF)] * 3,
        compiler_params=pltpu.CompilerParams(vmem_limit_bytes=50 * 2**20),
        cost_estimate=pl.CostEstimate(
            flops=12 * rows * width * half * 128, bytes_accessed=16 * 2**20, transcendentals=0
        ),
    )(x, dy, mixing, *pieces)


def weight_grads_kernel(way, x, dy, hg, gg, ug, sent, kept):
    for k, (left, right) in enumerate(((x, gg), (x, ug), (dy, hg))):
        grad = t_mm(left[...], right[...]).astype(BF)
        for core in range(2):
            for i in range(2):
                for j in range(2):
                    place = core * 4 + i * 2 + j
                    slot = (1 - j) * 2 + 1 - i if way == 0 else (1 - i) * 2 + 1 - j
                    for e in range(2):
                        (sent if core else kept)[slot, k, e] = grad[
                            place * 128 : (place + 1) * 128, e * 128 : (e + 1) * 128
                        ]


def weight_grads(way, x, dy, hg, gg, ug):
    rows, width = x.shape
    half = hg.shape[1] // 128
    whole = pl.BlockSpec((rows, width), lambda i: (0, 0))
    tile = pl.BlockSpec((rows, 256), lambda i: (0, i))
    quad = pl.BlockSpec((4, 3, 2, 128, 128), lambda i: (0, 0, i, 0, 0))
    return pl.pallas_call(
        functools.partial(weight_grads_kernel, way),
        grid=(half // 2,),
        in_specs=[whole, whole, tile, tile, tile],
        out_specs=[quad, quad],
        out_shape=[jax.ShapeDtypeStruct((4, 3, half, 128, 128), BF)] * 2,
        compiler_params=pltpu.CompilerParams(vmem_limit_bytes=50 * 2**20),
        cost_estimate=pl.CostEstimate(
            flops=6 * rows * width * half * 128, bytes_accessed=10 * 2**20, transcendentals=0
        ),
    )(x, dy, hg, gg, ug)


WAYS = ((2, 4), (4, 2))


def sum_near(way, sent, kept):
    core = swap(sent, "dp", 1)
    first = swap(add_low(kept[:2], core[:2]), "dp", WAYS[way][0])
    return kept[2:], core[2:], first


def sum_far(way, terms):
    kept, core, first = (t.astype(F32) for t in terms)
    held = kept + core + first
    return held[1] + swap(held[0].astype(BF), "dp", WAYS[way][1]).astype(F32)


def gather_rows(shards):
    ways = [(2, 4) if i % 2 == 0 else (4, 2) for i in range(len(shards))]
    if lax.axis_size("dp") != 8:
        return [lax.all_gather(s, "dp", axis=0, tiled=True) for s in shards]
    first = [swap(s, "dp", w[0]) for s, w in zip(shards, ways)]
    pairs = [jnp.stack([s, f]) for s, f in zip(shards, first)]
    second = [swap(p, "dp", w[1]) for p, w in zip(pairs, ways)]
    quads = [
        jnp.stack([p, s], axis=0 if w[1] == 4 else 1) for p, s, w in zip(pairs, second, ways)
    ]
    third = [swap(q, "dp", 1) for q in quads]
    return [
        jnp.concatenate([q, t]).reshape(-1, q.shape[-1]) for q, t in zip(quads, third)
    ]


def add_low(a, b):
    return (a.astype(F32) + b.astype(F32)).astype(BF)


def scatter_rows(full, way):
    if lax.axis_size("dp") != 8:
        return lax.psum_scatter(full, "dp", scatter_dimension=0, tiled=True).astype(F32)
    columns = full.shape[1]
    quads = full.reshape(2, 2, 2, 128, columns)
    other = swap(quads[1], "dp", 1)
    held = add_low(quads[0], other)
    if way == 0:
        pair = add_low(held[:, 0], swap(held[:, 1], "dp", 2))
        last = swap(pair[1], "dp", 4)
    else:
        pair = add_low(held[0], swap(held[1], "dp", 4))
        last = swap(pair[1], "dp", 2)
    return pair[0].astype(F32) + last.astype(F32)


def total(value):
    for axis in ("dp", "tensor"):
        bit = 1
        while bit < lax.axis_size(axis):
            value = value + swap(value, axis, bit)
            bit *= 2
    return value


def gather_tokens(rows):
    me = lax.axis_index("tensor")
    size = lax.axis_size("tensor")
    held = jnp.stack([rows] + [swap(rows, "tensor", r) for r in range(1, size)])
    return jnp.concatenate(
        [lax.dynamic_index_in_dim(held, me ^ b, 0, keepdims=False) for b in range(size)]
    )


def scatter_tokens(full):
    me = lax.axis_index("tensor")
    size = lax.axis_size("tensor")
    blocks = full.reshape(size, -1, full.shape[-1])
    out = lax.dynamic_index_in_dim(blocks, me, 0, keepdims=False).astype(F32)
    for r in range(1, size):
        piece = lax.dynamic_index_in_dim(blocks, me ^ r, 0, keepdims=False)
        out = out + swap(piece, "tensor", r).astype(F32)
    return out


def rows_first(weight):
    return jnp.swapaxes(weight, 0, 1).reshape(weight.shape[1], -1)


def experts_first(grad, experts):
    return jnp.swapaxes(grad.reshape(grad.shape[0], experts, -1), 0, 1)


def local(
    residual_in,
    norm1_gain,
    w_query,
    key_weight,
    value_weight,
    w_out,
    norm2_gain,
    w_gate,
    w_up,
    w_down,
    expert_ids,
    gate_weights,
    out_grad,
):
    group_rows = expert_ids.shape[0]
    sequences = group_rows // LEN
    heads_q = w_query.shape[1] // HEAD_SIZE
    heads_kv = key_weight.shape[1] // HEAD_SIZE
    per_kv = heads_q // heads_kv
    experts = w_gate.shape[0]
    factor_s = HEAD_SIZE ** (-0.5)
    bf_type = jnp.bfloat16
    f_type = jnp.float32
    relative = lax.axis_size("dp") == 8
    q_width, k_width = w_query.shape[1], key_weight.shape[1]
    residual, cotangent, gain_one, gain_two = reorder(
        (residual_in, out_grad, norm1_gain[None, :], norm2_gain[None, :]), False
    )
    residual = residual.astype(f_type)
    gain_one, gain_two = gain_one[0], gain_two[0]
    full_qk, full_vo = gather_rows(
        [
            jnp.concatenate([w_query, key_weight], axis=1),
            jnp.concatenate([value_weight, w_out], axis=1),
        ]
    )
    full_v, full_o = full_vo[:, :k_width], full_vo[:, k_width:]
    factor_one = rms_factor(residual)
    normed = lax.all_gather(
        (residual * factor_one * gain_one).astype(bf_type), "tensor", axis=0, tiled=True
    )
    half = experts // 2
    parts = (slice(0, half), slice(half, None))
    if relative:
        shards = [jnp.stack([w_gate[p], w_up[p], w_down[p]]) for p in parts]
        firsts = [swap(w, "dp", way[0]) for w, way in zip(shards, WAYS)]
        pairs = [jnp.stack([w, f]) for w, f in zip(shards, firsts)]
        seconds = [swap(p, "dp", way[1]) for p, way in zip(pairs, WAYS)]
    else:
        shards = [
            jnp.concatenate([rows_first(w_gate[p]), rows_first(w_up[p])], axis=1) for p in parts
        ] + [rows_first(w_down[p]) for p in parts]
        shards, full_qk = lax.optimization_barrier((shards, full_qk))
        gu_a, gu_b, d_a, d_b = gather_rows(shards)
    later, normed = lax.optimization_barrier((cotangent, normed))
    grad_rows = gather_tokens(later)
    cosine_table, sine_table = rope_tables(LEN, HEAD_SIZE)
    cosine_table = cosine_table[:, None, :]
    sine_table = sine_table[:, None, :]
    qk_raw = mm(normed, full_qk)
    query_raw = qk_raw[:, :q_width].reshape(sequences, LEN, heads_q, HEAD_SIZE)
    query = apply_rotary(query_raw, cosine_table, sine_table).astype(bf_type)
    keys_raw = qk_raw[:, q_width:].reshape(sequences, LEN, heads_kv, HEAD_SIZE)
    key_rows = apply_rotary(keys_raw, cosine_table, sine_table).astype(bf_type)
    value_rows = mm(normed, full_v).astype(bf_type).reshape(sequences, LEN, heads_kv, HEAD_SIZE)
    causal = jnp.arange(LEN)[:, None] >= jnp.arange(LEN)[None, :]

    def score_block(query_seq, key_seq):
        grouped = query_seq.reshape(LEN, heads_kv, per_kv, HEAD_SIZE)
        scores = (
            jnp.einsum("qkgd,skd->kgqs", grouped, key_seq, preferred_element_type=f_type) * factor_s
        )
        return jnp.where(causal, scores, -1e30)

    def forward_one(pieces):
        query_seq, key_seq, value_seq = pieces
        scores = score_block(query_seq, key_seq)
        row_max = jnp.max(scores, axis=-1, keepdims=True)
        exp_scores = jnp.exp(scores - row_max)
        row_sum = jnp.sum(exp_scores, axis=-1, keepdims=True)
        chances = (exp_scores / row_sum).astype(bf_type)
        attended = jnp.einsum("kgqs,skd->qkgd", chances, value_seq, preferred_element_type=f_type)
        return (attended.reshape(LEN, heads_q * HEAD_SIZE), (row_max + jnp.log(row_sum))[..., 0])

    attended, log_sums = lax.map(forward_one, (query, key_rows, value_rows))
    heads_out = attended.reshape(group_rows, heads_q * HEAD_SIZE).astype(bf_type)
    middle = residual + lax.psum_scatter(
        mm_t(heads_out, full_o).astype(bf_type), "tensor", scatter_dimension=0, tiled=True
    ).astype(f_type)
    factor_two = rms_factor(middle)
    normed_two_rows = (middle * factor_two * gain_two).astype(bf_type)
    normed_two = lax.all_gather(normed_two_rows, "tensor", axis=0, tiled=True)
    chosen = expert_ids[:, :, None] == jnp.arange(experts, dtype=jnp.int32)[None, None, :]
    mixing = jnp.sum(jnp.where(chosen, gate_weights[:, :, None], 0.0), axis=1)
    if relative:
        pairs, seconds, _ = lax.optimization_barrier((pairs, seconds, normed_two_rows))
        results = []
        for way in range(2):
            pieces = (pairs[way], seconds[way], swap(pairs[way], "dp", 1))
            pieces = pieces + (swap(seconds[way], "dp", 1),)
            results.append(experts_part(way, normed_two, grad_rows, mixing, pieces))
        normed_two_part = results[0][0] + results[1][0]
        mixed_part = results[0][1] + results[1][1]
    else:
        mixed_part, normed_two_part, low_grads = 0.0, 0.0, []
        for mix, gu, down in ((mixing[:, :half], gu_a, d_a), (mixing[:, half:], gu_b, d_b)):
            width = down.shape[1]
            spread = jnp.broadcast_to(
                mix[:, :, None], (group_rows, half, width // half)
            ).reshape(group_rows, width)
            both = mm(normed_two, gu)
            gate_proj, up_proj = both[:, :width], both[:, width:]
            sigmoid_g = jax.nn.sigmoid(gate_proj)
            activated = gate_proj * sigmoid_g
            hidden = (activated * up_proj * spread).astype(bf_type)
            hidden_grad = mm(grad_rows, down) * spread
            gate_grad = hidden_grad * up_proj * sigmoid_g * (1.0 + gate_proj * (1.0 - sigmoid_g))
            up_grad = hidden_grad * activated
            both_grad = jnp.concatenate([gate_grad.astype(bf_type), up_grad.astype(bf_type)], axis=1)
            normed_two_part = normed_two_part + mm_t(both_grad, gu)
            mixed_part = mixed_part + mm_t(hidden, down)
            low_grads.append((both_grad, hidden))
    normed_two_grad = lax.psum_scatter(
        normed_two_part.astype(bf_type), "tensor", scatter_dimension=0, tiled=True
    ).astype(f_type)
    if relative:
        sums = []
        for way in range(2):
            sent, kept = weight_grads(way, normed_two, grad_rows, *results[way][2:])
            sums.append(sum_near(way, sent, kept))
    else:
        gu_grads, down_grads = [], []
        for way, (both_grad, hidden) in enumerate(low_grads):
            gu_grads.append(scatter_rows(t_mm(normed_two, both_grad).astype(bf_type), way))
            down_grads.append(scatter_rows(t_mm(grad_rows, hidden).astype(bf_type), way))
        width = down_grads[0].shape[1]
        w_gate_grad = jnp.concatenate([experts_first(g[:, :width], half) for g in gu_grads])
        w_up_grad = jnp.concatenate([experts_first(g[:, width:], half) for g in gu_grads])
        w_down_grad = jnp.concatenate([experts_first(g, half) for g in down_grads])
    back_two, gain_two_part = norm_back(middle, factor_two, gain_two, normed_two_grad)
    middle_grad = cotangent.astype(f_type) + back_two
    middle_rows = lax.all_gather(middle_grad.astype(bf_type), "tensor", axis=0, tiled=True)
    mixed_low, middle_rows = lax.optimization_barrier((mixed_part.astype(bf_type), middle_rows))
    residual_out = (middle + scatter_tokens(mixed_low)).astype(bf_type)
    grad_out_w = t_mm(middle_rows, heads_out)
    heads_grad = jnp.dot(middle_rows, full_o, preferred_element_type=f_type).astype(bf_type)
    heads_grad = heads_grad.reshape(sequences, LEN, heads_q * HEAD_SIZE)

    def backward_one(pieces):
        query_seq, key_seq, value_seq, log_seq, grad_seq = pieces
        scores = score_block(query_seq, key_seq)
        chances = jnp.exp(scores - log_seq[..., None])
        grad_grouped = grad_seq.reshape(LEN, heads_kv, per_kv, HEAD_SIZE)
        grad_value = jnp.einsum(
            "kgqs,qkgd->skd", chances.astype(bf_type), grad_grouped, preferred_element_type=f_type
        )
        grad_chances = jnp.einsum(
            "qkgd,skd->kgqs", grad_grouped, value_seq, preferred_element_type=f_type
        )
        grad_scores = (
            chances * (grad_chances - jnp.sum(grad_chances * chances, axis=-1, keepdims=True))
        ).astype(bf_type)
        grad_query = (
            jnp.einsum("kgqs,skd->qkgd", grad_scores, key_seq, preferred_element_type=f_type)
            * factor_s
        )
        grouped = query_seq.reshape(LEN, heads_kv, per_kv, HEAD_SIZE)
        grad_key = (
            jnp.einsum("kgqs,qkgd->skd", grad_scores, grouped, preferred_element_type=f_type)
            * factor_s
        )
        return (grad_query.reshape(LEN, heads_q, HEAD_SIZE), grad_key, grad_value)

    query_rgrad, keys_rgrad, values_rgrad = lax.map(
        backward_one, (query, key_rows, value_rows, log_sums, heads_grad)
    )
    if relative:
        sums, query_rgrad, keys_rgrad, values_rgrad = lax.optimization_barrier(
            (sums, query_rgrad, keys_rgrad, values_rgrad)
        )
        sums = [sum_far(way, sums[way]) for way in range(2)]
        w_gate_grad, w_up_grad, w_down_grad = (
            jnp.concatenate([sums[0][k], sums[1][k]]) for k in range(3)
        )
    query_grad = (
        rotate_back(query_rgrad, cosine_table, sine_table)
        .astype(bf_type)
        .reshape(group_rows, heads_q * HEAD_SIZE)
    )
    keys_grad = (
        rotate_back(keys_rgrad, cosine_table, sine_table)
        .astype(bf_type)
        .reshape(group_rows, heads_kv * HEAD_SIZE)
    )
    values_grad = values_rgrad.astype(bf_type).reshape(group_rows, heads_kv * HEAD_SIZE)
    qk_grad = jnp.concatenate([query_grad, keys_grad], axis=1)
    grad_qk_w = scatter_rows(t_mm(normed, qk_grad).astype(bf_type), 0)
    grad_vo_w = scatter_rows(
        jnp.concatenate([t_mm(normed, values_grad), grad_out_w], axis=1).astype(bf_type), 1
    )
    w_query_grad, w_key_grad = grad_qk_w[:, :q_width], grad_qk_w[:, q_width:]
    w_value_grad, w_out_grad = grad_vo_w[:, :k_width], grad_vo_w[:, k_width:]
    normed_part = mm_t(qk_grad, full_qk) + mm_t(values_grad, full_v)
    gain_one_part = jnp.sum(normed_part * normed.astype(f_type), axis=0) / gain_one
    (gains,) = reorder((jnp.stack([gain_one_part, gain_two_part]),), True)
    gains = total(gains)
    normed_grad = lax.psum_scatter(
        normed_part.astype(bf_type), "tensor", scatter_dimension=0, tiled=True
    ).astype(f_type)
    back_one, _ = norm_back(residual, factor_one, gain_one, normed_grad)
    residual_out, input_grad = reorder((residual_out, middle_grad + back_one), True)
    norm1_gain_grad, norm2_gain_grad = gains[0], gains[1]
    return (
        residual_out,
        input_grad,
        norm1_gain_grad,
        w_query_grad,
        w_key_grad,
        w_value_grad,
        w_out_grad,
        norm2_gain_grad,
        w_gate_grad,
        w_up_grad,
        w_down_grad,
    )


def solution(mesh):
    placed = (
        P(("dp", "tensor"), None),
        P(),
        P("dp", "tensor"),
        P("dp", "tensor"),
        P("dp", "tensor"),
        P("dp", "tensor"),
        P(),
        P(None, "dp", "tensor"),
        P(None, "dp", "tensor"),
        P(None, "dp", "tensor"),
        P("dp", None),
        P("dp", None),
        P(("dp", "tensor"), None),
    )
    return jax.shard_map(
        local,
        mesh=mesh,
        in_specs=placed,
        out_specs=(
            P(("dp", "tensor"), None),
            P(("dp", "tensor"), None),
            P(),
            P("dp", "tensor"),
            P("dp", "tensor"),
            P("dp", "tensor"),
            P("dp", "tensor"),
            P(),
            P(None, "dp", "tensor"),
            P(None, "dp", "tensor"),
            P(None, "dp", "tensor"),
        ),
        check_vma=False,
    )
```
